32 devices in a mesh: turn: 4 (over y, core), line: 8 (over z, x).
Axes of the slice: x: 2, y: 2, z: 4, core: 2. Of those that a mesh axis runs over, the one named last changes fastest.
Arguments:
- turn_regret: float32 [16, 8, 1326], P('turn'), may hold values from -6 to 6
- river_regret: float32 [16, 24, 8, 8, 1326], P('turn', 'line'), may hold values from -6 to 6
- opp_reach: float32 [16, 1326], P('turn'), may hold values from 0.1 to 1
- trav_reach: bfloat16 [16, 8, 1326], P('turn'), may hold values from 0 to 1
- pot: float32 [8, 8], replicated, may hold values from 1 to 8
- blockers: int32 [16, 24, 1326], P('turn', 'line'), may hold values 0 or 1
- ranks: int32 [16, 24, 1326], P('turn', 'line'), may hold values from 0 to 7461
Outputs:
- new_turn_regret: float32 [16, 8, 1326], P('turn')
- new_river_regret: float32 [16, 24, 8, 8, 1326], P('turn', 'line')
- root_value: float32 [1326], replicated
The draws below stay inside these ranges and needn't reach their ends.
All inputs are finite; a program needn't handle non-finite values. No bound on the sum of `blockers` on one device may be relied on, other than what follows from the above.
Results may differ from the reference program's by a relative error of at most 0.0003.
Values sent between devices are 32-bit elements; how exact they have to be, the bound alone decides.
A program may use at most 64 MiB of HBM per device.

```python
import math
import jax
import jax.numpy as jnp
import numpy as np
from jax import lax

CARDS = 52
HANDS = 1326
LINES = 8
TREES = 16
RIVERS = 24


def plant(drawn, key, low, high):
    dims = drawn.shape
    place = [jax.random.randint(jax.random.fold_in(key, axis), (), 0, dims[axis]) for axis in range(len(dims))]
    drawn = drawn.at[tuple(place)].set(low)
    longest = dims.index(max(dims))
    place[longest] = (place[longest] + 1) % dims[longest]
    return drawn.at[tuple(place)].set(high)


def levels(rng, extent, split, low, high):
    def one(dim, shards_of):
        heights = jax.random.uniform(jax.random.fold_in(jax.random.fold_in(rng, 6), dim), (shards_of,), jnp.float32, low / len(split), high / len(split))
        return jnp.repeat(jnp.exp(heights), extent[dim] // shards_of).reshape((-1,) + (1,) * (len(extent) - dim - 1))

    loudness = one(*split[0])
    for cut in split[1:]:
        loudness = loudness * one(*cut)
    return loudness


def gaussian(stream_key, shape, deviation, limit, shards=(), held_as=jnp.bfloat16):
    result = jax.random.normal(stream_key, shape, jnp.float32) * deviation
    if len(shards) > 0:
        result = levels(stream_key, shape, shards, -0.22, 0.18) * result
    return jnp.clip(result, min=-limit, max=limit).astype(held_as)


def setup_inputs(seed: int = 0) -> dict:
    keys = jax.random.split(jax.random.key(seed), 8)
    return {
        "turn_regret": gaussian(keys[0], (TREES, LINES, HANDS), 1.0, 6.0, ((0, 4),), jnp.float32),
        "river_regret": gaussian(keys[1], (TREES, RIVERS, LINES, LINES, HANDS), 1.0, 6.0, ((0, 4), (1, 8)), jnp.float32),
        "opp_reach": jnp.clip(0.1 + 0.9 * jax.random.uniform(keys[2], (TREES, HANDS), jnp.float32) ** levels(keys[2], (TREES, HANDS), ((0, 4),), -0.2, 0.2), 0.1, 1.0),
        "trav_reach": jnp.clip(1.0 * jax.random.uniform(keys[3], (TREES, LINES, HANDS), jnp.float32) ** levels(keys[3], (TREES, LINES, HANDS), ((0, 4),), -0.2, 0.2), 0.0, 1.0).astype(jnp.bfloat16),
        "pot": jnp.clip(jnp.exp(jax.random.uniform(keys[4], (LINES, LINES), jnp.float32, math.log(1.0), math.log(8.0))), 1.0, 8.0),
        "blockers": plant((jax.random.randint(keys[5], (TREES, RIVERS, HANDS), 0, 13) < 12).astype(jnp.int32), jax.random.fold_in(keys[5], 1), 0, 1),
        "ranks": plant(jax.random.randint(keys[6], (TREES, RIVERS, HANDS), 0, 7462), jax.random.fold_in(keys[6], 1), 0, 7461).astype(jnp.int32),
    }


POS_KEEP = 0.99718
NEG_KEEP = 0.5


def regret_match(regret, reduce_axis):
    positive = jnp.maximum(regret, 0.0)
    positive_sum = jnp.sum(positive, axis=reduce_axis, keepdims=True)
    uniform = 1.0 / regret.shape[reduce_axis]
    safe_sum = jnp.where(positive_sum > 0, positive_sum, 1.0)
    return jnp.where(positive_sum > 0, positive / safe_sum, uniform)


def discount(regret):
    return jnp.where(regret > 0, regret * POS_KEEP, regret * NEG_KEEP)


def card_pairs(card_count):
    card_low, card_high = np.triu_indices(card_count, 1)
    return jnp.asarray(card_low.astype(np.int32)), jnp.asarray(card_high.astype(np.int32))


def showdown_matrix(rank_row, card_low, card_high):
    clash = (card_low[:, None] == card_low[None, :]) | (card_low[:, None] == card_high[None, :])
    clash = clash | (card_high[:, None] == card_low[None, :]) | (card_high[:, None] == card_high[None, :])
    verdict = jnp.sign(rank_row[:, None] - rank_row[None, :])
    return jnp.where(clash, 0, verdict).astype(jnp.bfloat16)


def runout(reach_pair, regrets, blocked, rank_row, pot, card_low, card_high):
    hand_count = rank_row.shape[0]
    line_count = pot.shape[0]
    unblocked = blocked.astype(jnp.float32)
    strategy = regret_match(regrets, 1)
    opp_part = reach_pair[0].astype(jnp.float32)
    trav_part = reach_pair[1].astype(jnp.float32)
    weighted = jnp.sum(pot[:, :, None] * strategy, axis=1)
    opp_weight = (opp_part * unblocked * weighted).astype(jnp.bfloat16)
    trav_weight = (trav_part * unblocked).astype(jnp.bfloat16)
    stacked = jnp.concatenate([opp_weight, trav_weight], 0)
    showdown = showdown_matrix(rank_row, card_low, card_high)
    product = jnp.einsum("ch,gh->cg", stacked.astype(jnp.float32), showdown.astype(jnp.float32))
    trav_value = unblocked * product[:line_count] / hand_count
    opp_gain = unblocked * product[line_count:] / hand_count
    action_value = pot[:, :, None] * opp_gain[:, None, :]
    node_value = jnp.sum(strategy * action_value, axis=1)
    updated = discount(regrets) + action_value - node_value[:, None, :]
    return updated, jnp.stack([trav_value, node_value])


def reference(turn_regret, river_regret, opp_reach, trav_reach, pot, blockers, ranks):
    card_low, card_high = card_pairs(CARDS)
    turn_strategy = regret_match(turn_regret, 1)
    opp_lines = (opp_reach[:, None, :] * turn_strategy).astype(jnp.bfloat16)
    reach_pairs = jnp.stack([opp_lines, trav_reach], 1)

    def per_tree(tree_items):
        reach_pair, regrets, blocked, rank_rows = tree_items

        def per_river(river_items):
            return runout(reach_pair, river_items[0], river_items[1], river_items[2], pot, card_low, card_high)

        return lax.map(per_river, (regrets, blocked, rank_rows))

    new_river_regret, values = lax.map(per_tree, (reach_pairs, river_regret, blockers, ranks))
    returned = jnp.sum(values, axis=1) / RIVERS
    line_gain = returned[:, 1]
    node_turn = jnp.sum(turn_strategy * line_gain, axis=1)
    new_turn_regret = discount(turn_regret) + line_gain - node_turn[:, None, :]
    root_value = jnp.sum(trav_reach.astype(jnp.float32) * returned[:, 0], axis=(0, 1)) / TREES
    return new_turn_regret, new_river_regret, root_value
```

```python
import functools
import math

import jax
import jax.numpy as jnp
import numpy as np
from jax import lax
from jax.experimental import pallas as pl
from jax.experimental.pallas import tpu as pltpu
from jax.sharding import PartitionSpec as P

POS_KEEP = 0.99718
NEG_KEEP = 0.5
LANE = 128


def regret_match(regret, reduce_axis):
    positive = jnp.maximum(regret, 0.0)
    positive_sum = jnp.sum(positive, axis=reduce_axis, keepdims=True)
    uniform = 1.0 / regret.shape[reduce_axis]
    safe_sum = jnp.where(positive_sum > 0, positive_sum, 1.0)
    return jnp.where(positive_sum > 0, positive / safe_sum, uniform)


def discount(regret):
    return jnp.maximum(regret * POS_KEEP, regret * NEG_KEEP)


def incidence(hands, padded):
    cards = (1 + math.isqrt(1 + 8 * hands)) // 2
    low, high = np.triu_indices(cards, 1)
    table = np.zeros((padded, LANE), np.float32)
    table[np.arange(hands), low] = 1.0
    table[np.arange(hands), high] = 1.0
    return table


def runout_kernel(
    hands, rivers,
    pot_smem, inc_ref, inc_t_ref, regret_ref, turn_ref, opp_ref, trav_ref, blk_ref, rank_ref,
    out_ref, node_ref, root_ref,
    upper, lower, potb, stacked, phi, col, wgt, prod, root_acc,
):
    tree, river = pl.program_id(0), pl.program_id(1)
    padded = upper.shape[0]
    lines = pot_smem.shape[0]
    first = jnp.logical_and(tree == 0, river == 0)

    @pl.when(first)
    def _():
        stacked[...] = jnp.zeros_like(stacked)
        phi[...] = jnp.zeros_like(phi)
        root_acc[...] = jnp.zeros_like(root_acc)
        row = lax.broadcasted_iota(jnp.int32, (lines, LANE), 0)
        for l in range(lines):
            plane = jnp.zeros((lines, LANE), jnp.float32)
            for m in range(lines):
                plane = jnp.where(row == m, pot_smem[l, m], plane)
            potb[l] = plane
        for start in range(0, padded, LANE):
            rows = pl.ds(start, LANE)
            shared = jnp.dot(inc_ref[rows, :], inc_t_ref[...], preferred_element_type=jnp.float32)
            free = (1.0 - jnp.minimum(shared, 1.0)).astype(jnp.bfloat16)
            upper[rows, :] = free
            lower[rows, :] = -free

    unblocked = blk_ref[0, pl.ds(river, 1), :].astype(jnp.float32)
    rank = rank_ref[0, pl.ds(river, 1), :]
    value = ((rank & 127) + 128).astype(jnp.float32)
    for bit in range(6):
        value = jnp.where((rank & (128 << bit)) != 0, value * float(2 ** (2**bit)), value)
    phi[:, :hands] = jnp.broadcast_to(value, (8, hands))
    col[...] = jnp.broadcast_to(phi[0:1, :], (LANE, padded)).T.astype(jnp.bfloat16)

    turn_strategy = regret_match(turn_ref[0], 0)
    opp_lines = (opp_ref[pl.ds(tree, 1), :] * turn_strategy).astype(jnp.bfloat16)
    opp_part = opp_lines.astype(jnp.float32) * unblocked
    trav = trav_ref[0].astype(jnp.float32)
    for start in range(0, hands, LANE):
        width = min(LANE, hands - start)
        at = pl.ds(start, width)
        pos = jnp.maximum(regret_ref[0, 0, :, :, at], 0.0)
        total = jnp.sum(pos, axis=1)
        potted = jnp.sum(pos * potb[:, :, :width], axis=1)
        mean_pot = jnp.sum(potb[:, :, :width], axis=1) / lines
        some = total > 0
        wgt[:, at] = jnp.where(some, potted / jnp.where(some, total, 1.0), mean_pot)
    weighted = wgt[:, :hands]
    both = jnp.concatenate([opp_part * weighted, trav * unblocked], axis=0)
    stacked[:, :hands] = both.astype(jnp.bfloat16)

    row_phi = [jnp.broadcast_to(phi[:, pl.ds(j, LANE)], (8, LANE)).astype(jnp.bfloat16)[0:1] for j in range(0, padded, LANE)]
    deep = 256
    for n0 in range(0, padded, deep):
        nw = min(deep, padded - n0)
        acc = jnp.zeros((2 * lines, nw), jnp.float32)
        for k0 in range(0, padded, deep):
            kw = min(deep, padded - k0)
            rows = pl.ds(k0, kw)
            parts = []
            for j in range(n0, n0 + nw, LANE):
                gap = row_phi[j // LANE] - col[rows, :]
                cols = pl.ds(j, LANE)
                parts.append(jnp.maximum(jnp.minimum(gap, upper[rows, cols]), lower[rows, cols]))
            acc = acc + jnp.dot(stacked[:, rows], jnp.concatenate(parts, axis=1), preferred_element_type=jnp.float32)
        prod[:, pl.ds(n0, nw)] = acc

    scaled = unblocked / hands
    root_acc[...] += trav * scaled * prod[:lines, :hands]
    gain = scaled * prod[lines:, :hands]
    node = gain * weighted

    @pl.when(river == 0)
    def _():
        node_ref[0] = node

    @pl.when(river > 0)
    def _():
        node_ref[0] += node

    for l in range(lines):
        for start in range(0, hands, LANE):
            width = min(LANE, hands - start)
            at = slice(start, start + width)
            plane = discount(regret_ref[0, 0, l, :, at]) + potb[l, :, :width] * gain[l : l + 1, at]
            out_ref[0, 0, l, :, at] = plane - node[l : l + 1, at]

    @pl.when(jnp.logical_and(tree == pl.num_programs(0) - 1, river == rivers - 1))
    def _():
        root_ref[...] = jnp.sum(root_acc[...], axis=0, keepdims=True)


def run_local(turn_regret, river_regret, opp_reach, trav_reach, pot, blockers, ranks):
    trees, rivers, lines, _, hands = river_regret.shape
    padded = -(-hands // LANE) * LANE
    table = incidence(hands, padded)
    inc, inc_t = jnp.asarray(table, jnp.bfloat16), jnp.asarray(table.T, jnp.bfloat16)
    bf, f32 = jnp.bfloat16, jnp.float32
    per_tree = lambda s, r: (s, 0, 0)
    whole = lambda s, r: (0, 0)
    return pl.pallas_call(
        functools.partial(runout_kernel, hands, rivers),
        grid=(trees, rivers),
        out_shape=(
            jax.ShapeDtypeStruct(river_regret.shape, f32),
            jax.ShapeDtypeStruct((trees, lines, hands), f32),
            jax.ShapeDtypeStruct((1, hands), f32),
        ),
        in_specs=[
            pl.BlockSpec(memory_space=pltpu.SMEM),
            pl.BlockSpec((padded, LANE), whole),
            pl.BlockSpec((LANE, padded), whole),
            pl.BlockSpec((1, 1, lines, lines, hands), lambda s, r: (s, r, 0, 0, 0)),
            pl.BlockSpec((1, lines, hands), per_tree),
            pl.BlockSpec((trees, hands), whole),
            pl.BlockSpec((1, lines, hands), per_tree),
            pl.BlockSpec((1, rivers, hands), per_tree),
            pl.BlockSpec((1, rivers, hands), per_tree),
        ],
        out_specs=(
            pl.BlockSpec((1, 1, lines, lines, hands), lambda s, r: (s, r, 0, 0, 0)),
            pl.BlockSpec((1, lines, hands), per_tree),
            pl.BlockSpec((1, hands), whole),
        ),
        scratch_shapes=[
            pltpu.VMEM((padded, padded), bf),
            pltpu.VMEM((padded, padded), bf),
            pltpu.VMEM((lines, lines, LANE), f32),
            pltpu.VMEM((2 * lines, padded), bf),
            pltpu.VMEM((8, padded), f32),
            pltpu.VMEM((padded, LANE), bf),
            pltpu.VMEM((lines, padded), f32),
            pltpu.VMEM((2 * lines, padded), f32),
            pltpu.VMEM((lines, hands), f32),
        ],
        compiler_params=pltpu.CompilerParams(vmem_limit_bytes=48 * 2**20),
    )(pot, inc, inc_t, river_regret, turn_regret, opp_reach, trav_reach, blockers, ranks)


def body(turn_regret, river_regret, opp_reach, trav_reach, pot, blockers, ranks):
    river_count = river_regret.shape[1] * lax.axis_size("line")
    tree_count = turn_regret.shape[0] * lax.axis_size("turn")
    new_river_regret, node_sum, root = run_local(
        turn_regret, river_regret, opp_reach, trav_reach, pot, blockers, ranks
    )
    line_gain = lax.psum(node_sum, "line") / river_count
    root_value = lax.psum(root[0], ("turn", "line")) / (tree_count * river_count)
    turn_strategy = regret_match(turn_regret, 1)
    node_turn = jnp.sum(turn_strategy * line_gain, axis=1)
    new_turn_regret = discount(turn_regret) + line_gain - node_turn[:, None, :]
    return (new_turn_regret, new_river_regret, root_value)


def solution(mesh):
    in_specs = (
        P("turn", None, None),
        P("turn", "line", None, None, None),
        P("turn", None),
        P("turn", None, None),
        P(),
        P("turn", "line", None),
        P("turn", "line", None),
    )
    out_specs = (P("turn", None, None), P("turn", "line", None, None, None), P())
    return jax.shard_map(body, mesh=mesh, in_specs=in_specs, out_specs=out_specs, check_vma=False)
```

```python
import functools
import math

import jax
import jax.numpy as jnp
import numpy as np
from jax import lax
from jax.experimental import pallas as pl
from jax.experimental.pallas import tpu as pltpu
from jax.sharding import PartitionSpec as P

POS_KEEP = 0.99718
NEG_KEEP = 0.5
LANE = 128


def regret_match(regret, reduce_axis):
    positive = jnp.maximum(regret, 0.0)
    positive_sum = jnp.sum(positive, axis=reduce_axis, keepdims=True)
    uniform = 1.0 / regret.shape[reduce_axis]
    safe_sum = jnp.where(positive_sum > 0, positive_sum, 1.0)
    return jnp.where(positive_sum > 0, positive / safe_sum, uniform)


def discount(regret):
    return jnp.maximum(regret * POS_KEEP, regret * NEG_KEEP)


def incidence(hands, padded):
    cards = (1 + math.isqrt(1 + 8 * hands)) // 2
    low, high = np.triu_indices(cards, 1)
    table = np.zeros((padded, LANE), np.float32)
    table[np.arange(hands), low] = 1.0
    table[np.arange(hands), high] = 1.0
    return table


def runout_kernel(
    hands, rivers,
    pot_smem, inc_ref, regret_ref, turn_ref, opp_ref, trav_ref, code_ref,
    out_ref, node_ref, root_ref,
    upper, lower, potb, stacked, phi, col, wgt, prod, root_acc,
):
    tree, river = pl.program_id(0), pl.program_id(1)
    padded = upper.shape[0]
    lines = pot_smem.shape[0]
    first = jnp.logical_and(tree == 0, river == 0)

    @pl.when(first)
    def _():
        stacked[...] = jnp.zeros_like(stacked)
        phi[...] = jnp.zeros_like(phi)
        root_acc[...] = jnp.zeros_like(root_acc)
        row = lax.broadcasted_iota(jnp.int32, (lines, LANE), 0)
        for l in range(lines):
            plane = jnp.zeros((lines, LANE), jnp.float32)
            for m in range(lines):
                plane = jnp.where(row == m, pot_smem[l, m], plane)
            potb[l] = plane
        for start in range(0, padded, LANE):
            rows = pl.ds(start, LANE)
            shared = lax.dot_general(
                inc_ref[rows, :], inc_ref[...], (((1,), (1,)), ((), ())),
                preferred_element_type=jnp.float32,
            )
            free = (1.0 - jnp.minimum(shared, 1.0)).astype(jnp.bfloat16)
            upper[rows, :] = free
            lower[rows, :] = -free

    code = code_ref[0, pl.ds(river, 1), :]
    unblocked = (code & 1).astype(jnp.float32)
    rank = code >> 1
    value = ((rank & 127) + 128).astype(jnp.float32)
    for bit in range(6):
        value = jnp.where((rank & (128 << bit)) != 0, value * float(2 ** (2**bit)), value)
    phi[:, :hands] = jnp.broadcast_to(value, (8, hands))
    col[...] = jnp.broadcast_to(phi[0:1, :], (LANE, padded)).T.astype(jnp.bfloat16)

    turn_strategy = regret_match(turn_ref[0], 0)
    opp_lines = (opp_ref[pl.ds(tree, 1), :] * turn_strategy).astype(jnp.bfloat16)
    opp_part = opp_lines.astype(jnp.float32) * unblocked
    trav = trav_ref[0].astype(jnp.float32)
    for start in range(0, hands, LANE):
        width = min(LANE, hands - start)
        at = pl.ds(start, width)
        pos = jnp.maximum(regret_ref[0, 0, :, :, at], 0.0)
        total = jnp.sum(pos, axis=1)
        potted = jnp.sum(pos * potb[:, :, :width], axis=1)
        mean_pot = jnp.sum(potb[:, :, :width], axis=1) / lines
        some = total > 0
        wgt[:, at] = jnp.where(some, potted / jnp.where(some, total, 1.0), mean_pot)
    weighted = wgt[:, :hands]
    both = jnp.concatenate([opp_part * weighted, trav * unblocked], axis=0)
    stacked[:, :hands] = both.astype(jnp.bfloat16)

    row_phi = [jnp.broadcast_to(phi[:, pl.ds(j, LANE)], (8, LANE)).astype(jnp.bfloat16)[0:1] for j in range(0, padded, LANE)]
    deep = 256
    for n0 in range(0, padded, deep):
        nw = min(deep, padded - n0)
        acc = jnp.zeros((2 * lines, nw), jnp.float32)
        for k0 in range(0, padded, deep):
            kw = min(deep, padded - k0)
            rows = pl.ds(k0, kw)
            parts = []
            for j in range(n0, n0 + nw, LANE):
                gap = row_phi[j // LANE] - col[rows, :]
                cols = pl.ds(j, LANE)
                parts.append(jnp.maximum(jnp.minimum(gap, upper[rows, cols]), lower[rows, cols]))
            acc = acc + jnp.dot(stacked[:, rows], jnp.concatenate(parts, axis=1), preferred_element_type=jnp.float32)
        prod[:, pl.ds(n0, nw)] = acc

    scaled = unblocked / hands
    root_acc[...] += trav * scaled * prod[:lines, :hands]
    gain = scaled * prod[lines:, :hands]
    node = gain * weighted

    @pl.when(river == 0)
    def _():
        node_ref[0] = node

    @pl.when(river > 0)
    def _():
        node_ref[0] += node

    for l in range(lines):
        for start in range(0, hands, LANE):
            width = min(LANE, hands - start)
            at = slice(start, start + width)
            plane = discount(regret_ref[0, 0, l, :, at]) + potb[l, :, :width] * gain[l : l + 1, at]
            out_ref[0, 0, l, :, at] = plane - node[l : l + 1, at]

    @pl.when(jnp.logical_and(tree == pl.num_programs(0) - 1, river == rivers - 1))
    def _():
        root_ref[...] = jnp.sum(root_acc[...], axis=0, keepdims=True)


def run_local(turn_regret, river_regret, opp_reach, trav_reach, pot, blockers, ranks):
    trees, rivers, lines, _, hands = river_regret.shape
    padded = -(-hands // LANE) * LANE
    table = incidence(hands, padded)
    inc = jnp.asarray(table, jnp.bfloat16)
    codes = jnp.pad(ranks * 2 + blockers, ((0, 0), (0, -rivers % 8), (0, 0)))
    bf, f32 = jnp.bfloat16, jnp.float32
    per_tree = lambda s, r: (s, 0, 0)
    whole = lambda s, r: (0, 0)
    return pl.pallas_call(
        functools.partial(runout_kernel, hands, rivers),
        grid=(trees, rivers),
        out_shape=(
            jax.ShapeDtypeStruct(river_regret.shape, f32),
            jax.ShapeDtypeStruct((trees, lines, hands), f32),
            jax.ShapeDtypeStruct((1, hands), f32),
        ),
        in_specs=[
            pl.BlockSpec(memory_space=pltpu.SMEM),
            pl.BlockSpec((padded, LANE), whole),
            pl.BlockSpec((1, 1, lines, lines, hands), lambda s, r: (s, r, 0, 0, 0)),
            pl.BlockSpec((1, lines, hands), per_tree),
            pl.BlockSpec((trees, hands), whole),
            pl.BlockSpec((1, lines, hands), per_tree),
            pl.BlockSpec((1, codes.shape[1], hands), per_tree),
        ],
        out_specs=(
            pl.BlockSpec((1, 1, lines, lines, hands), lambda s, r: (s, r, 0, 0, 0)),
            pl.BlockSpec((1, lines, hands), per_tree),
            pl.BlockSpec((1, hands), whole),
        ),
        scratch_shapes=[
            pltpu.VMEM((padded, padded), bf),
            pltpu.VMEM((padded, padded), bf),
            pltpu.VMEM((lines, lines, LANE), f32),
            pltpu.VMEM((2 * lines, padded), bf),
            pltpu.VMEM((8, padded), f32),
            pltpu.VMEM((padded, LANE), bf),
            pltpu.VMEM((lines, padded), f32),
            pltpu.VMEM((2 * lines, padded), f32),
            pltpu.VMEM((lines, hands), f32),
        ],
        compiler_params=pltpu.CompilerParams(vmem_limit_bytes=60 * 2**20),
    )(pot, inc, river_regret, turn_regret, opp_reach, trav_reach, codes)


def combine_kernel(
    line_size, turn_size, river_count, tree_count,
    node_ref, root_ref, turn_ref, out_ref, value_ref,
    outbox, inbox, total, gather, root_total, root_box, gain,
    send1, recv1, send2, recv2, send3, recv3,
):
    me, mine = lax.axis_index("line"), lax.axis_index("turn")
    line_peers = [lax.rem(me + i, line_size) for i in range(1, line_size)]
    turn_peers = [lax.rem(mine + i, turn_size) for i in range(1, turn_size)]
    mesh_ids = pl.DeviceIdType.MESH
    barrier = pltpu.get_barrier_semaphore()
    for peer in line_peers:
        pl.semaphore_signal(barrier, inc=1, device_id=(mine, peer), device_id_type=mesh_ids)
    for peer in turn_peers:
        pl.semaphore_signal(barrier, inc=1, device_id=(peer, me), device_id_type=mesh_ids)

    trees, lines, hands = node_ref.shape
    rows = trees * lines // line_size
    tiles = -(-hands // LANE)
    spans = [(j, min(LANE, hands - j * LANE)) for j in range(tiles)]
    outbox[...] = jnp.zeros_like(outbox)
    gain[...] = jnp.zeros_like(gain)
    for j, width in spans:
        at = pl.ds(j * LANE, width)
        for d in range(line_size):
            tree, line = divmod(d * rows, lines)
            outbox[d, pl.ds(j * rows, rows), :width] = node_ref[tree, pl.ds(line, rows), at]
            outbox[d, pl.ds(tiles * rows + j, 1), :width] = root_ref[:, at]
    pl.semaphore_wait(barrier, line_size + turn_size - 2)

    firsts = []
    for peer in line_peers:
        copy = pltpu.make_async_remote_copy(
            src_ref=outbox.at[peer], dst_ref=inbox.at[me], send_sem=send1.at[peer],
            recv_sem=recv1.at[me], device_id=(mine, peer), device_id_type=mesh_ids,
        )
        copy.start()
        firsts.append(copy)
    inbox[me] = outbox[me]
    for peer in line_peers:
        pltpu.make_async_remote_copy(
            src_ref=outbox.at[peer], dst_ref=inbox.at[peer], send_sem=send1.at[peer],
            recv_sem=recv1.at[peer], device_id=(mine, peer), device_id_type=mesh_ids,
        ).wait_recv()
    summed = inbox[0]
    for d in range(1, line_size):
        summed = summed + inbox[d]
    total[...] = summed[: total.shape[0]]
    root_total[...] = jnp.zeros_like(root_total)
    root_total[:tiles, :] = summed[tiles * rows : tiles * rows + tiles]

    seconds = []
    for peer in line_peers:
        copy = pltpu.make_async_remote_copy(
            src_ref=total, dst_ref=gather.at[me], send_sem=send2.at[peer],
            recv_sem=recv2.at[me], device_id=(mine, peer), device_id_type=mesh_ids,
        )
        copy.start()
        seconds.append(copy)
    for peer in turn_peers:
        copy = pltpu.make_async_remote_copy(
            src_ref=root_total, dst_ref=root_box.at[mine], send_sem=send3.at[peer],
            recv_sem=recv3.at[mine], device_id=(peer, me), device_id_type=mesh_ids,
        )
        copy.start()
        seconds.append(copy)
    gather[me] = total[...]
    root_box[mine] = root_total[...]
    for peer in line_peers:
        pltpu.make_async_remote_copy(
            src_ref=total, dst_ref=gather.at[peer], send_sem=send2.at[peer],
            recv_sem=recv2.at[peer], device_id=(mine, peer), device_id_type=mesh_ids,
        ).wait_recv()
    for j, width in spans:
        for d in range(line_size):
            tree, line = divmod(d * rows, lines)
            gain[tree, pl.ds(line, rows), pl.ds(j * LANE, LANE)] = gather[d, pl.ds(j * rows, rows), :]
    for tree in range(trees):
        regret = turn_ref[tree]
        line_gain = gain[tree, :, :hands] / river_count
        average = jnp.sum(regret_match(regret, 0) * line_gain, axis=0, keepdims=True)
        out_ref[tree] = discount(regret) + line_gain - average
    for peer in turn_peers:
        pltpu.make_async_remote_copy(
            src_ref=root_total, dst_ref=root_box.at[peer], send_sem=send3.at[peer],
            recv_sem=recv3.at[peer], device_id=(peer, me), device_id_type=mesh_ids,
        ).wait_recv()
    value = root_box[0]
    for d in range(1, turn_size):
        value = value + root_box[d]
    value = value / (river_count * tree_count)
    for j, width in spans:
        value_ref[:, pl.ds(j * LANE, width)] = value[j : j + 1, :width]
    for copy in firsts + seconds:
        copy.wait_send()


def combine(node_sum, root, turn_regret, river_count, tree_count):
    trees, lines, hands = node_sum.shape
    line_size, turn_size = lax.axis_size("line"), lax.axis_size("turn")
    tiles = -(-hands // LANE)
    rows = trees * lines // line_size
    up8 = lambda n: -(-n // 8) * 8
    message, share, root_rows = up8(tiles * (rows + 1)), up8(tiles * rows), up8(tiles)
    f32, dma = jnp.float32, pltpu.SemaphoreType.DMA
    vmem = pl.BlockSpec(memory_space=pltpu.VMEM)
    return pl.pallas_call(
        functools.partial(combine_kernel, line_size, turn_size, river_count, tree_count),
        out_shape=(
            jax.ShapeDtypeStruct((trees, lines, hands), f32),
            jax.ShapeDtypeStruct((1, hands), f32),
        ),
        in_specs=[vmem] * 3,
        out_specs=(vmem, vmem),
        scratch_shapes=[
            pltpu.VMEM((line_size, message, LANE), f32),
            pltpu.VMEM((line_size, message, LANE), f32),
            pltpu.VMEM((share, LANE), f32),
            pltpu.VMEM((line_size, share, LANE), f32),
            pltpu.VMEM((root_rows, LANE), f32),
            pltpu.VMEM((turn_size, root_rows, LANE), f32),
            pltpu.VMEM((trees, lines, tiles * LANE), f32),
            dma((line_size,)), dma((line_size,)),
            dma((line_size,)), dma((line_size,)),
            dma((turn_size,)), dma((turn_size,)),
        ],
        compiler_params=pltpu.CompilerParams(
            collective_id=0, has_side_effects=True, vmem_limit_bytes=16 * 2**20
        ),
    )(node_sum, root, turn_regret)


def body(turn_regret, river_regret, opp_reach, trav_reach, pot, blockers, ranks):
    river_count = river_regret.shape[1] * lax.axis_size("line")
    tree_count = turn_regret.shape[0] * lax.axis_size("turn")
    new_river_regret, node_sum, root = run_local(
        turn_regret, river_regret, opp_reach, trav_reach, pot, blockers, ranks
    )
    new_turn_regret, root_value = combine(node_sum, root, turn_regret, river_count, tree_count)
    return (new_turn_regret, new_river_regret, root_value[0])


def solution(mesh):
    in_specs = (
        P("turn", None, None),
        P("turn", "line", None, None, None),
        P("turn", None),
        P("turn", None, None),
        P(),
        P("turn", "line", None),
        P("turn", "line", None),
    )
    out_specs = (P("turn", None, None), P("turn", "line", None, None, None), P())
    return jax.shard_map(body, mesh=mesh, in_specs=in_specs, out_specs=out_specs, check_vma=False)
```

```python
import functools
import math

import jax
import jax.numpy as jnp
import numpy as np
from jax import lax
from jax.experimental import pallas as pl
from jax.experimental.pallas import tpu as pltpu
from jax.sharding import PartitionSpec as P

POS_KEEP = 0.99718
NEG_KEEP = 0.5
LANE = 128


def regret_match(regret, reduce_axis):
    positive = jnp.maximum(regret, 0.0)
    positive_sum = jnp.sum(positive, axis=reduce_axis, keepdims=True)
    uniform = 1.0 / regret.shape[reduce_axis]
    safe_sum = jnp.where(positive_sum > 0, positive_sum, 1.0)
    return jnp.where(positive_sum > 0, positive / safe_sum, uniform)


def discount(regret):
    return jnp.maximum(regret * POS_KEEP, regret * NEG_KEEP)


def incidence(hands, padded):
    cards = (1 + math.isqrt(1 + 8 * hands)) // 2
    low, high = np.triu_indices(cards, 1)
    table = np.zeros((padded, LANE), np.float32)
    table[np.arange(hands), low] = 1.0
    table[np.arange(hands), high] = 1.0
    return table


def runout_kernel(
    hands, rivers, steps,
    pot_smem, inc_ref, regret_ref, next_ref, turn_ref, opp_ref, trav_ref, blk_ref, rank_ref,
    out_ref, node_ref, root_ref,
    upper, lower, potb, stacked, wgt, stacked_next, wgt_next, phi, col, root_acc,
):
    step = pl.program_id(0)
    tree, river = step // rivers, lax.rem(step, rivers)
    padded = upper.shape[0]
    lines = pot_smem.shape[0]
    deep = 256

    def rows_of(at_step):
        at_tree = pl.ds(at_step // rivers, 1)
        unblocked = blk_ref[lax.rem(at_step, rivers), at_tree, :].astype(jnp.float32)
        return unblocked, opp_ref[at_tree, :]

    def prepare(at_step, row_pair, source, start):
        width = min(LANE, hands - start)
        at = pl.ds(start, width)
        at_tree = at_step // rivers
        unblocked, opp = (row[:, start : start + width] for row in row_pair)
        turn_strategy = regret_match(turn_ref[at_tree, :, at], 0)
        opp_lines = (opp * turn_strategy).astype(jnp.bfloat16)
        pos = jnp.maximum(source[0, :, :, at], 0.0)
        total = jnp.sum(pos, axis=1)
        potted = jnp.sum(pos * potb[:, :, :width], axis=1)
        mean_pot = jnp.sum(potb[:, :, :width], axis=1) / lines
        some = total > 0
        weighted = jnp.where(some, potted / jnp.where(some, total, 1.0), mean_pot)
        wgt_next[:, at] = weighted
        trav = trav_ref[at_tree, :, at].astype(jnp.float32) * unblocked
        both = jnp.concatenate([opp_lines.astype(jnp.float32) * unblocked * weighted, trav], axis=0)
        stacked_next[:, at] = both.astype(jnp.bfloat16)

    @pl.when(step == 0)
    def _():
        stacked_next[...] = jnp.zeros_like(stacked_next)
        phi[...] = jnp.zeros_like(phi)
        root_acc[...] = jnp.zeros_like(root_acc)
        row = lax.broadcasted_iota(jnp.int32, (lines, LANE), 0)
        for l in range(lines):
            plane = jnp.zeros((lines, LANE), jnp.float32)
            for m in range(lines):
                plane = jnp.where(row == m, pot_smem[l, m], plane)
            potb[l] = plane
        for start in range(0, padded, LANE):
            rows = pl.ds(start, LANE)
            shared = lax.dot_general(
                inc_ref[rows, :], inc_ref[...], (((1,), (1,)), ((), ())),
                preferred_element_type=jnp.float32,
            )
            free = (1.0 - jnp.minimum(shared, 1.0)).astype(jnp.bfloat16)
            upper[rows, :] = free
            lower[rows, :] = -free
        for start in range(0, hands, LANE):
            prepare(0, rows_of(jnp.int32(0)), regret_ref, start)

    stacked[...] = stacked_next[...]
    wgt[...] = wgt_next[...]

    @pl.when(river == 0)
    def _():
        node_ref[...] = jnp.zeros_like(node_ref)

    rank = rank_ref[river, pl.ds(tree, 1), :]
    value = ((rank & 127) + 128).astype(jnp.float32)
    for bit in range(6):
        value = jnp.where((rank & (128 << bit)) != 0, value * float(2 ** (2**bit)), value)
    phi[:, :hands] = jnp.broadcast_to(value, (8, hands))
    col[...] = jnp.broadcast_to(phi[0:1, :], (LANE, padded)).T.astype(jnp.bfloat16)

    following = jnp.minimum(step + 1, steps - 1)
    next_rows = rows_of(following)
    scale = rows_of(step)[0] / hands
    for n0 in range(0, padded, deep):
        nw = min(deep, padded - n0)
        row_phi = [phi[0:1, pl.ds(j, LANE)].astype(jnp.bfloat16) for j in range(n0, n0 + nw, LANE)]
        acc = jnp.zeros((2 * lines, nw), jnp.float32)
        for k0 in range(0, padded, deep):
            rows = pl.ds(k0, min(deep, padded - k0))
            parts = []
            for j in range(nw // LANE):
                gap = row_phi[j] - col[rows, :]
                cols = pl.ds(n0 + j * LANE, LANE)
                parts.append(jnp.maximum(jnp.minimum(gap, upper[rows, cols]), lower[rows, cols]))
            tile = jnp.concatenate(parts, axis=1)
            acc = acc + jnp.dot(stacked[:, rows], tile, preferred_element_type=jnp.float32)
        for start in range(n0, n0 + nw, LANE):
            prepare(following, next_rows, next_ref, start)
            width = min(LANE, hands - start)
            at = pl.ds(start, width)
            product = acc[:, start - n0 : start - n0 + width]
            scaled = scale[:, start : start + width]
            root_acc[:, at] += trav_ref[tree, :, at].astype(jnp.float32) * scaled * product[:lines]
            gain = scaled * product[lines:]
            node = gain * wgt[:, at]
            node_ref[0, :, at] += node
            for l in range(lines):
                plane = discount(regret_ref[0, l, :, at]) + potb[l, :, :width] * gain[l : l + 1]
                out_ref[0, l, :, at] = plane - node[l : l + 1]

    @pl.when(step == steps - 1)
    def _():
        root_ref[...] = jnp.sum(root_acc[...], axis=0, keepdims=True)


def run_local(turn_regret, river_regret, opp_reach, trav_reach, pot, blockers, ranks):
    trees, rivers, lines, _, hands = river_regret.shape
    steps = trees * rivers
    padded = -(-hands // LANE) * LANE
    inc = jnp.asarray(incidence(hands, padded), jnp.bfloat16)
    regrets = river_regret.reshape(steps, lines, lines, hands)
    bf, f32 = jnp.bfloat16, jnp.float32
    block = (1, lines, lines, hands)
    outs = pl.pallas_call(
        functools.partial(runout_kernel, hands, rivers, steps),
        grid=(steps,),
        out_shape=(
            jax.ShapeDtypeStruct(regrets.shape, f32),
            jax.ShapeDtypeStruct((trees, lines, hands), f32),
            jax.ShapeDtypeStruct((1, hands), f32),
        ),
        in_specs=[
            pl.BlockSpec(memory_space=pltpu.SMEM),
            pl.BlockSpec((padded, LANE), lambda i: (0, 0)),
            pl.BlockSpec(block, lambda i: (i, 0, 0, 0)),
            pl.BlockSpec(block, lambda i: (jnp.minimum(i + 1, steps - 1), 0, 0, 0)),
            pl.BlockSpec((trees, lines, hands), lambda i: (0, 0, 0)),
            pl.BlockSpec((trees, hands), lambda i: (0, 0)),
            pl.BlockSpec((trees, lines, hands), lambda i: (0, 0, 0)),
            pl.BlockSpec((rivers, trees, hands), lambda i: (0, 0, 0)),
            pl.BlockSpec((rivers, trees, hands), lambda i: (0, 0, 0)),
        ],
        out_specs=(
            pl.BlockSpec(block, lambda i: (i, 0, 0, 0)),
            pl.BlockSpec((1, lines, hands), lambda i: (i // rivers, 0, 0)),
            pl.BlockSpec((1, hands), lambda i: (0, 0)),
        ),
        scratch_shapes=[
            pltpu.VMEM((padded, padded), bf),
            pltpu.VMEM((padded, padded), bf),
            pltpu.VMEM((lines, lines, LANE), f32),
            pltpu.VMEM((2 * lines, padded), bf),
            pltpu.VMEM((lines, padded), f32),
            pltpu.VMEM((2 * lines, padded), bf),
            pltpu.VMEM((lines, padded), f32),
            pltpu.VMEM((8, padded), f32),
            pltpu.VMEM((padded, LANE), bf),
            pltpu.VMEM((lines, hands), f32),
        ],
        compiler_params=pltpu.CompilerParams(vmem_limit_bytes=60 * 2**20),
    )(pot, inc, regrets, regrets, turn_regret, opp_reach, trav_reach,
      blockers.transpose(1, 0, 2), ranks.transpose(1, 0, 2))
    return (outs[0].reshape(river_regret.shape),) + tuple(outs[1:])


def combine_kernel(
    line_size, turn_size, river_count, tree_count,
    node_hbm, root_hbm, turn_ref, out_ref, value_ref,
    node_ref, root_ref, in_sem, outbox, inbox, total, gather, root_total, root_box, gain,
    send1, recv1, send2, recv2, send3, recv3,
):
    me, mine = lax.axis_index("line"), lax.axis_index("turn")
    line_peers = [lax.rem(me + i, line_size) for i in range(1, line_size)]
    turn_peers = [lax.rem(mine + i, turn_size) for i in range(1, turn_size)]
    mesh_ids = pl.DeviceIdType.MESH
    loads = [
        pltpu.make_async_copy(node_hbm, node_ref, in_sem.at[0]),
        pltpu.make_async_copy(root_hbm, root_ref, in_sem.at[1]),
    ]
    for load in loads:
        load.start()
    barrier = pltpu.get_barrier_semaphore()
    for peer in line_peers:
        pl.semaphore_signal(barrier, inc=1, device_id=(mine, peer), device_id_type=mesh_ids)
    for peer in turn_peers:
        pl.semaphore_signal(barrier, inc=1, device_id=(peer, me), device_id_type=mesh_ids)

    trees, lines, hands = node_ref.shape
    rows = trees * lines // line_size
    tiles = -(-hands // LANE)
    spans = [(j, min(LANE, hands - j * LANE)) for j in range(tiles)]
    outbox[...] = jnp.zeros_like(outbox)
    gain[...] = jnp.zeros_like(gain)
    for load in loads:
        load.wait()
    for j, width in spans:
        at = pl.ds(j * LANE, width)
        for d in range(line_size):
            tree, line = divmod(d * rows, lines)
            outbox[d, pl.ds(j * rows, rows), :width] = node_ref[tree, pl.ds(line, rows), at]
            outbox[d, pl.ds(tiles * rows + j, 1), :width] = root_ref[:, at]
    pl.semaphore_wait(barrier, line_size + turn_size - 2)

    firsts = []
    for peer in line_peers:
        copy = pltpu.make_async_remote_copy(
            src_ref=outbox.at[peer], dst_ref=inbox.at[me], send_sem=send1.at[peer],
            recv_sem=recv1.at[me], device_id=(mine, peer), device_id_type=mesh_ids,
        )
        copy.start()
        firsts.append(copy)
    inbox[me] = outbox[me]
    for peer in line_peers:
        pltpu.make_async_remote_copy(
            src_ref=outbox.at[peer], dst_ref=inbox.at[peer], send_sem=send1.at[peer],
            recv_sem=recv1.at[peer], device_id=(mine, peer), device_id_type=mesh_ids,
        ).wait_recv()
    summed = inbox[0]
    for d in range(1, line_size):
        summed = summed + inbox[d]
    total[...] = summed[: total.shape[0]]
    root_total[...] = jnp.zeros_like(root_total)
    root_total[:tiles, :] = summed[tiles * rows : tiles * rows + tiles]

    seconds = []
    for peer in line_peers:
        copy = pltpu.make_async_remote_copy(
            src_ref=total, dst_ref=gather.at[me], send_sem=send2.at[peer],
            recv_sem=recv2.at[me], device_id=(mine, peer), device_id_type=mesh_ids,
        )
        copy.start()
        seconds.append(copy)
    for peer in turn_peers:
        copy = pltpu.make_async_remote_copy(
            src_ref=root_total, dst_ref=root_box.at[mine], send_sem=send3.at[peer],
            recv_sem=recv3.at[mine], device_id=(peer, me), device_id_type=mesh_ids,
        )
        copy.start()
        seconds.append(copy)
    gather[me] = total[...]
    root_box[mine] = root_total[...]
    for peer in line_peers:
        pltpu.make_async_remote_copy(
            src_ref=total, dst_ref=gather.at[peer], send_sem=send2.at[peer],
            recv_sem=recv2.at[peer], device_id=(mine, peer), device_id_type=mesh_ids,
        ).wait_recv()
    for j, width in spans:
        for d in range(line_size):
            tree, line = divmod(d * rows, lines)
            gain[tree, pl.ds(line, rows), pl.ds(j * LANE, LANE)] = gather[d, pl.ds(j * rows, rows), :]
    for tree in range(trees):
        regret = turn_ref[tree]
        line_gain = gain[tree, :, :hands] / river_count
        average = jnp.sum(regret_match(regret, 0) * line_gain, axis=0, keepdims=True)
        out_ref[tree] = discount(regret) + line_gain - average
    for peer in turn_peers:
        pltpu.make_async_remote_copy(
            src_ref=root_total, dst_ref=root_box.at[peer], send_sem=send3.at[peer],
            recv_sem=recv3.at[peer], device_id=(peer, me), device_id_type=mesh_ids,
        ).wait_recv()
    value = root_box[0]
    for d in range(1, turn_size):
        value = value + root_box[d]
    value = value / (river_count * tree_count)
    for j, width in spans:
        value_ref[:, pl.ds(j * LANE, width)] = value[j : j + 1, :width]
    for copy in firsts + seconds:
        copy.wait_send()


def combine(node_sum, root, turn_regret, river_count, tree_count):
    trees, lines, hands = node_sum.shape
    line_size, turn_size = lax.axis_size("line"), lax.axis_size("turn")
    tiles = -(-hands // LANE)
    rows = trees * lines // line_size
    up8 = lambda n: -(-n // 8) * 8
    message, share, root_rows = up8(tiles * (rows + 1)), up8(tiles * rows), up8(tiles)
    f32, dma = jnp.float32, pltpu.SemaphoreType.DMA
    vmem = pl.BlockSpec(memory_space=pltpu.VMEM)
    return pl.pallas_call(
        functools.partial(combine_kernel, line_size, turn_size, river_count, tree_count),
        out_shape=(
            jax.ShapeDtypeStruct((trees, lines, hands), f32),
            jax.ShapeDtypeStruct((1, hands), f32),
        ),
        in_specs=[pl.BlockSpec(memory_space=pl.ANY)] * 2 + [vmem],
        out_specs=(vmem, vmem),
        scratch_shapes=[
            pltpu.VMEM((trees, lines, hands), f32),
            pltpu.VMEM((1, hands), f32),
            dma((2,)),
            pltpu.VMEM((line_size, message, LANE), f32),
            pltpu.VMEM((line_size, message, LANE), f32),
            pltpu.VMEM((share, LANE), f32),
            pltpu.VMEM((line_size, share, LANE), f32),
            pltpu.VMEM((root_rows, LANE), f32),
            pltpu.VMEM((turn_size, root_rows, LANE), f32),
            pltpu.VMEM((trees, lines, tiles * LANE), f32),
            dma((line_size,)), dma((line_size,)),
            dma((line_size,)), dma((line_size,)),
            dma((turn_size,)), dma((turn_size,)),
        ],
        compiler_params=pltpu.CompilerParams(
            collective_id=0, has_side_effects=True, vmem_limit_bytes=60 * 2**20
        ),
    )(node_sum, root, turn_regret)


def body(turn_regret, river_regret, opp_reach, trav_reach, pot, blockers, ranks):
    river_count = river_regret.shape[1] * lax.axis_size("line")
    tree_count = turn_regret.shape[0] * lax.axis_size("turn")
    new_river_regret, node_sum, root = run_local(
        turn_regret, river_regret, opp_reach, trav_reach, pot, blockers, ranks
    )
    new_turn_regret, root_value = combine(node_sum, root, turn_regret, river_count, tree_count)
    return (new_turn_regret, new_river_regret, root_value[0])


def solution(mesh):
    in_specs = (
        P("turn", None, None),
        P("turn", "line", None, None, None),
        P("turn", None),
        P("turn", None, None),
        P(),
        P("turn", "line", None),
        P("turn", "line", None),
    )
    out_specs = (P("turn", None, None), P("turn", "line", None, None, None), P())
    return jax.shard_map(body, mesh=mesh, in_specs=in_specs, out_specs=out_specs, check_vma=False)
```

```python
import functools
import math

import jax
import jax.numpy as jnp
import numpy as np
from jax import lax
from jax.experimental import pallas as pl
from jax.experimental.pallas import tpu as pltpu
from jax.sharding import PartitionSpec as P

POS_KEEP = 0.99718
NEG_KEEP = 0.5
LANE = 128


def regret_match(regret, reduce_axis):
    positive = jnp.maximum(regret, 0.0)
    positive_sum = jnp.sum(positive, axis=reduce_axis, keepdims=True)
    uniform = 1.0 / regret.shape[reduce_axis]
    safe_sum = jnp.where(positive_sum > 0, positive_sum, 1.0)
    return jnp.where(positive_sum > 0, positive / safe_sum, uniform)


def discount(regret):
    return jnp.maximum(regret * POS_KEEP, regret * NEG_KEEP)


def incidence(hands, padded):
    cards = (1 + math.isqrt(1 + 8 * hands)) // 2
    low, high = np.triu_indices(cards, 1)
    table = np.zeros((padded, LANE), np.float32)
    table[np.arange(hands), low] = 1.0
    table[np.arange(hands), high] = 1.0
    return table


def runout_kernel(
    hands, rivers, steps,
    pot_smem, inc_ref, regret_ref, next_ref, turn_ref, opp_ref, trav_ref, blk_ref, rank_ref,
    out_ref, node_ref, root_ref,
    upper, lower, potb, stacked, wgt, stacked_next, wgt_next, phi, col, root_acc,
):
    step = pl.program_id(0)
    tree, river = step // rivers, lax.rem(step, rivers)
    padded = upper.shape[0]
    lines = pot_smem.shape[0]
    deep = 256

    def rows_of(at_step):
        at_tree = pl.ds(at_step // rivers, 1)
        unblocked = blk_ref[lax.rem(at_step, rivers), at_tree, :].astype(jnp.float32)
        return unblocked, opp_ref[at_tree, :]

    def prepare(at_step, row_pair, source, start):
        width = min(LANE, hands - start)
        at = pl.ds(start, width)
        at_tree = at_step // rivers
        unblocked, opp = (row[:, start : start + width] for row in row_pair)
        turn_strategy = regret_match(turn_ref[at_tree, :, at], 0)
        opp_lines = (opp * turn_strategy).astype(jnp.bfloat16)
        pos = jnp.maximum(source[0, :, :, at], 0.0)
        total = jnp.sum(pos, axis=1)
        potted = jnp.sum(pos * potb[:, :, :width], axis=1)
        mean_pot = jnp.sum(potb[:, :, :width], axis=1) / lines
        some = total > 0
        weighted = jnp.where(some, potted / jnp.where(some, total, 1.0), mean_pot)
        wgt_next[:, at] = weighted
        trav = trav_ref[at_tree, :, at].astype(jnp.float32) * unblocked
        both = jnp.concatenate([opp_lines.astype(jnp.float32) * unblocked * weighted, trav], axis=0)
        stacked_next[:, at] = both.astype(jnp.bfloat16)

    @pl.when(step == 0)
    def _():
        stacked_next[...] = jnp.zeros_like(stacked_next)
        phi[...] = jnp.zeros_like(phi)
        root_acc[...] = jnp.zeros_like(root_acc)
        row = lax.broadcasted_iota(jnp.int32, (lines, LANE), 0)
        for l in range(lines):
            plane = jnp.zeros((lines, LANE), jnp.float32)
            for m in range(lines):
                plane = jnp.where(row == m, pot_smem[l, m], plane)
            potb[l] = plane
        for start in range(0, padded, LANE):
            rows = pl.ds(start, LANE)
            shared = lax.dot_general(
                inc_ref[rows, :], inc_ref[...], (((1,), (1,)), ((), ())),
                preferred_element_type=jnp.float32,
            )
            free = (1.0 - jnp.minimum(shared, 1.0)).astype(jnp.bfloat16)
            upper[rows, :] = free
            lower[rows, :] = -free
        for start in range(0, hands, LANE):
            prepare(0, rows_of(jnp.int32(0)), regret_ref, start)

    stacked[...] = stacked_next[...]
    wgt[...] = wgt_next[...]

    @pl.when(river == 0)
    def _():
        node_ref[...] = jnp.zeros_like(node_ref)

    rank = rank_ref[river, pl.ds(tree, 1), :]
    value = ((rank & 127) + 128).astype(jnp.float32)
    for bit in range(6):
        value = jnp.where((rank & (128 << bit)) != 0, value * float(2 ** (2**bit)), value)
    phi[:, :hands] = jnp.broadcast_to(value, (8, hands))
    col[...] = jnp.broadcast_to(phi[0:1, :], (LANE, padded)).T.astype(jnp.bfloat16)

    following = jnp.minimum(step + 1, steps - 1)
    next_rows = rows_of(following)
    scale = rows_of(step)[0] / hands
    for n0 in range(0, padded, deep):
        nw = min(deep, padded - n0)
        row_phi = [phi[0:1, pl.ds(j, LANE)].astype(jnp.bfloat16) for j in range(n0, n0 + nw, LANE)]
        acc = jnp.zeros((2 * lines, nw), jnp.float32)
        for k0 in range(0, padded, deep):
            rows = pl.ds(k0, min(deep, padded - k0))
            parts = []
            for j in range(nw // LANE):
                gap = row_phi[j] - col[rows, :]
                cols = pl.ds(n0 + j * LANE, LANE)
                parts.append(jnp.maximum(jnp.minimum(gap, upper[rows, cols]), lower[rows, cols]))
            tile = jnp.concatenate(parts, axis=1)
            acc = acc + jnp.dot(stacked[:, rows], tile, preferred_element_type=jnp.float32)
        for start in range(n0, n0 + nw, LANE):
            prepare(following, next_rows, next_ref, start)
            width = min(LANE, hands - start)
            at = pl.ds(start, width)
            product = acc[:, start - n0 : start - n0 + width]
            scaled = scale[:, start : start + width]
            root_acc[:, at] += trav_ref[tree, :, at].astype(jnp.float32) * scaled * product[:lines]
            gain = scaled * product[lines:]
            node = gain * wgt[:, at]
            node_ref[0, :, at] += node
            for l in range(lines):
                plane = discount(regret_ref[0, l, :, at]) + potb[l, :, :width] * gain[l : l + 1]
                out_ref[0, l, :, at] = plane - node[l : l + 1]

    @pl.when(step == steps - 1)
    def _():
        root_ref[...] = jnp.sum(root_acc[...], axis=0, keepdims=True)


def run_local(turn_regret, river_regret, opp_reach, trav_reach, pot, blockers, ranks):
    trees, rivers, lines, _, hands = river_regret.shape
    steps = trees * rivers
    padded = -(-hands // LANE) * LANE
    inc = jnp.asarray(incidence(hands, padded), jnp.bfloat16)
    regrets = river_regret.reshape(steps, lines, lines, hands)
    bf, f32 = jnp.bfloat16, jnp.float32
    block = (1, lines, lines, hands)
    outs = pl.pallas_call(
        functools.partial(runout_kernel, hands, rivers, steps),
        grid=(steps,),
        out_shape=(
            jax.ShapeDtypeStruct(regrets.shape, f32),
            jax.ShapeDtypeStruct((trees, lines, hands), f32),
            jax.ShapeDtypeStruct((1, hands), f32),
        ),
        in_specs=[
            pl.BlockSpec(memory_space=pltpu.SMEM),
            pl.BlockSpec((padded, LANE), lambda i: (0, 0)),
            pl.BlockSpec(block, lambda i: (i, 0, 0, 0)),
            pl.BlockSpec(block, lambda i: (jnp.minimum(i + 1, steps - 1), 0, 0, 0)),
            pl.BlockSpec((trees, lines, hands), lambda i: (0, 0, 0)),
            pl.BlockSpec((trees, hands), lambda i: (0, 0)),
            pl.BlockSpec((trees, lines, hands), lambda i: (0, 0, 0)),
            pl.BlockSpec((rivers, trees, hands), lambda i: (0, 0, 0)),
            pl.BlockSpec((rivers, trees, hands), lambda i: (0, 0, 0)),
        ],
        out_specs=(
            pl.BlockSpec(block, lambda i: (i, 0, 0, 0)),
            pl.BlockSpec((1, lines, hands), lambda i: (i // rivers, 0, 0)),
            pl.BlockSpec((1, hands), lambda i: (0, 0)),
        ),
        scratch_shapes=[
            pltpu.VMEM((padded, padded), bf),
            pltpu.VMEM((padded, padded), bf),
            pltpu.VMEM((lines, lines, LANE), f32),
            pltpu.VMEM((2 * lines, padded), bf),
            pltpu.VMEM((lines, padded), f32),
            pltpu.VMEM((2 * lines, padded), bf),
            pltpu.VMEM((lines, padded), f32),
            pltpu.VMEM((8, padded), f32),
            pltpu.VMEM((padded, LANE), bf),
            pltpu.VMEM((lines, hands), f32),
        ],
        compiler_params=pltpu.CompilerParams(vmem_limit_bytes=60 * 2**20),
    )(pot, inc, regrets, regrets, turn_regret, opp_reach, trav_reach,
      blockers.transpose(1, 0, 2), ranks.transpose(1, 0, 2))
    return (outs[0].reshape(river_regret.shape),) + tuple(outs[1:])


def combine_kernel(
    line_size, turn_size, river_count, tree_count,
    node_ref, root_ref, turn_ref, out_ref, value_ref,
    outbox, inbox, total, gather, root_total, root_box, gain,
    send1, recv1, send2, recv2, send3, recv3,
):
    me, mine = lax.axis_index("line"), lax.axis_index("turn")
    line_peers = [lax.rem(me + i, line_size) for i in range(1, line_size)]
    turn_peers = [lax.rem(mine + i, turn_size) for i in range(1, turn_size)]
    mesh_ids = pl.DeviceIdType.MESH
    barrier = pltpu.get_barrier_semaphore()
    for peer in line_peers:
        pl.semaphore_signal(barrier, inc=1, device_id=(mine, peer), device_id_type=mesh_ids)
    for peer in turn_peers:
        pl.semaphore_signal(barrier, inc=1, device_id=(peer, me), device_id_type=mesh_ids)

    trees, lines, hands = node_ref.shape
    rows = trees * lines // line_size
    tiles = -(-hands // LANE)
    spans = [(j, min(LANE, hands - j * LANE)) for j in range(tiles)]
    outbox[...] = jnp.zeros_like(outbox)
    gain[...] = jnp.zeros_like(gain)
    for j, width in spans:
        at = pl.ds(j * LANE, width)
        for d in range(line_size):
            tree, line = divmod(d * rows, lines)
            outbox[d, pl.ds(j * rows, rows), :width] = node_ref[tree, pl.ds(line, rows), at]
            outbox[d, pl.ds(tiles * rows + j, 1), :width] = root_ref[:, at]
    pl.semaphore_wait(barrier, line_size + turn_size - 2)

    firsts = []
    for peer in line_peers:
        copy = pltpu.make_async_remote_copy(
            src_ref=outbox.at[peer], dst_ref=inbox.at[me], send_sem=send1.at[peer],
            recv_sem=recv1.at[me], device_id=(mine, peer), device_id_type=mesh_ids,
        )
        copy.start()
        firsts.append(copy)
    inbox[me] = outbox[me]
    for peer in line_peers:
        pltpu.make_async_remote_copy(
            src_ref=outbox.at[peer], dst_ref=inbox.at[peer], send_sem=send1.at[peer],
            recv_sem=recv1.at[peer], device_id=(mine, peer), device_id_type=mesh_ids,
        ).wait_recv()
    summed = inbox[0]
    for d in range(1, line_size):
        summed = summed + inbox[d]
    total[...] = summed[: total.shape[0]]
    root_total[...] = jnp.zeros_like(root_total)
    root_total[:tiles, :] = summed[tiles * rows : tiles * rows + tiles]

    seconds = []
    for peer in line_peers:
        copy = pltpu.make_async_remote_copy(
            src_ref=total, dst_ref=gather.at[me], send_sem=send2.at[peer],
            recv_sem=recv2.at[me], device_id=(mine, peer), device_id_type=mesh_ids,
        )
        copy.start()
        seconds.append(copy)
    for peer in turn_peers:
        copy = pltpu.make_async_remote_copy(
            src_ref=root_total, dst_ref=root_box.at[mine], send_sem=send3.at[peer],
            recv_sem=recv3.at[mine], device_id=(peer, me), device_id_type=mesh_ids,
        )
        copy.start()
        seconds.append(copy)
    gather[me] = total[...]
    root_box[mine] = root_total[...]
    for peer in line_peers:
        pltpu.make_async_remote_copy(
            src_ref=total, dst_ref=gather.at[peer], send_sem=send2.at[peer],
            recv_sem=recv2.at[peer], device_id=(mine, peer), device_id_type=mesh_ids,
        ).wait_recv()
    for j, width in spans:
        for d in range(line_size):
            tree, line = divmod(d * rows, lines)
            gain[tree, pl.ds(line, rows), pl.ds(j * LANE, LANE)] = gather[d, pl.ds(j * rows, rows), :]
    for tree in range(trees):
        regret = turn_ref[tree]
        line_gain = gain[tree, :, :hands] / river_count
        average = jnp.sum(regret_match(regret, 0) * line_gain, axis=0, keepdims=True)
        out_ref[tree] = discount(regret) + line_gain - average
    for peer in turn_peers:
        pltpu.make_async_remote_copy(
            src_ref=root_total, dst_ref=root_box.at[peer], send_sem=send3.at[peer],
            recv_sem=recv3.at[peer], device_id=(peer, me), device_id_type=mesh_ids,
        ).wait_recv()
    value = root_box[0]
    for d in range(1, turn_size):
        value = value + root_box[d]
    value = value / (river_count * tree_count)
    for j, width in spans:
        value_ref[:, pl.ds(j * LANE, width)] = value[j : j + 1, :width]
    for copy in firsts + seconds:
        copy.wait_send()


def combine(node_sum, root, turn_regret, river_count, tree_count):
    trees, lines, hands = node_sum.shape
    line_size, turn_size = lax.axis_size("line"), lax.axis_size("turn")
    tiles = -(-hands // LANE)
    rows = trees * lines // line_size
    up8 = lambda n: -(-n // 8) * 8
    message, share, root_rows = up8(tiles * (rows + 1)), up8(tiles * rows), up8(tiles)
    f32, dma = jnp.float32, pltpu.SemaphoreType.DMA
    vmem = pl.BlockSpec(memory_space=pltpu.VMEM)
    return pl.pallas_call(
        functools.partial(combine_kernel, line_size, turn_size, river_count, tree_count),
        out_shape=(
            jax.ShapeDtypeStruct((trees, lines, hands), f32),
            jax.ShapeDtypeStruct((1, hands), f32),
        ),
        in_specs=[vmem] * 3,
        out_specs=(vmem, vmem),
        scratch_shapes=[
            pltpu.VMEM((line_size, message, LANE), f32),
            pltpu.VMEM((line_size, message, LANE), f32),
            pltpu.VMEM((share, LANE), f32),
            pltpu.VMEM((line_size, share, LANE), f32),
            pltpu.VMEM((root_rows, LANE), f32),
            pltpu.VMEM((turn_size, root_rows, LANE), f32),
            pltpu.VMEM((trees, lines, tiles * LANE), f32),
            dma((line_size,)), dma((line_size,)),
            dma((line_size,)), dma((line_size,)),
            dma((turn_size,)), dma((turn_size,)),
        ],
        compiler_params=pltpu.CompilerParams(
            collective_id=0, has_side_effects=True, vmem_limit_bytes=16 * 2**20
        ),
    )(node_sum, root, turn_regret)


def body(turn_regret, river_regret, opp_reach, trav_reach, pot, blockers, ranks):
    river_count = river_regret.shape[1] * lax.axis_size("line")
    tree_count = turn_regret.shape[0] * lax.axis_size("turn")
    new_river_regret, node_sum, root = run_local(
        turn_regret, river_regret, opp_reach, trav_reach, pot, blockers, ranks
    )
    new_turn_regret, root_value = combine(node_sum, root, turn_regret, river_count, tree_count)
    return (new_turn_regret, new_river_regret, root_value[0])


def solution(mesh):
    in_specs = (
        P("turn", None, None),
        P("turn", "line", None, None, None),
        P("turn", None),
        P("turn", None, None),
        P(),
        P("turn", "line", None),
        P("turn", "line", None),
    )
    out_specs = (P("turn", None, None), P("turn", "line", None, None, None), P())
    return jax.shard_map(body, mesh=mesh, in_specs=in_specs, out_specs=out_specs, check_vma=False)
```

```python
import functools
import math

import jax
import jax.numpy as jnp
import numpy as np
from jax import lax
from jax.experimental import pallas as pl
from jax.experimental.pallas import tpu as pltpu
from jax.sharding import PartitionSpec as P

POS_KEEP = 0.99718
NEG_KEEP = 0.5
LANE = 128


def regret_match(regret, reduce_axis):
    positive = jnp.maximum(regret, 0.0)
    positive_sum = jnp.sum(positive, axis=reduce_axis, keepdims=True)
    uniform = 1.0 / regret.shape[reduce_axis]
    safe_sum = jnp.where(positive_sum > 0, positive_sum, 1.0)
    return jnp.where(positive_sum > 0, positive / safe_sum, uniform)


def discount(regret):
    return jnp.maximum(regret * POS_KEEP, regret * NEG_KEEP)


def incidence(hands, padded):
    cards = (1 + math.isqrt(1 + 8 * hands)) // 2
    low, high = np.triu_indices(cards, 1)
    table = np.zeros((padded, LANE), np.float32)
    table[np.arange(hands), low] = 1.0
    table[np.arange(hands), high] = 1.0
    return table


def runout_kernel(
    hands, rivers, steps,
    pot_smem, inc_ref, regret_ref, next_ref, turn_ref, opp_ref, trav_ref, blk_ref, rank_ref,
    out_ref, node_ref, root_ref,
    upper, lower, potb, stacked, wgt, stacked_next, wgt_next, phi, col, root_acc,
):
    step = pl.program_id(0)
    tree, river = step // rivers, lax.rem(step, rivers)
    padded = upper.shape[0]
    lines = pot_smem.shape[0]
    deep = 256

    def rows_of(at_step):
        at_tree = pl.ds(at_step // rivers, 1)
        unblocked = blk_ref[lax.rem(at_step, rivers), at_tree, :].astype(jnp.float32)
        return unblocked, opp_ref[at_tree, :]

    def prepare(at_step, row_pair, source, start):
        width = min(LANE, hands - start)
        at = pl.ds(start, width)
        at_tree = at_step // rivers
        unblocked, opp = (row[:, start : start + width] for row in row_pair)
        turn_strategy = regret_match(turn_ref[at_tree, :, at], 0)
        opp_lines = (opp * turn_strategy).astype(jnp.bfloat16)
        pos = jnp.maximum(source[0, :, :, at], 0.0)
        total = jnp.sum(pos, axis=1)
        potted = jnp.sum(pos * potb[:, :, :width], axis=1)
        mean_pot = jnp.sum(potb[:, :, :width], axis=1) / lines
        some = total > 0
        weighted = jnp.where(some, potted / jnp.where(some, total, 1.0), mean_pot)
        wgt_next[:, at] = weighted
        trav = trav_ref[at_tree, :, at].astype(jnp.float32) * unblocked
        both = jnp.concatenate([opp_lines.astype(jnp.float32) * unblocked * weighted, trav], axis=0)
        stacked_next[:, at] = both.astype(jnp.bfloat16)

    @pl.when(step == 0)
    def _():
        stacked_next[...] = jnp.zeros_like(stacked_next)
        phi[...] = jnp.zeros_like(phi)
        root_acc[...] = jnp.zeros_like(root_acc)
        row = lax.broadcasted_iota(jnp.int32, (lines, LANE), 0)
        for l in range(lines):
            plane = jnp.zeros((lines, LANE), jnp.float32)
            for m in range(lines):
                plane = jnp.where(row == m, pot_smem[l, m], plane)
            potb[l] = plane
        for start in range(0, padded, LANE):
            rows = pl.ds(start, LANE)
            shared = lax.dot_general(
                inc_ref[rows, :], inc_ref[...], (((1,), (1,)), ((), ())),
                preferred_element_type=jnp.float32,
            )
            free = (1.0 - jnp.minimum(shared, 1.0)).astype(jnp.bfloat16)
            upper[rows, :] = free
            lower[rows, :] = -free
        for start in range(0, hands, LANE):
            prepare(0, rows_of(jnp.int32(0)), regret_ref, start)

    stacked[...] = stacked_next[...]
    wgt[...] = wgt_next[...]

    @pl.when(river == 0)
    def _():
        node_ref[...] = jnp.zeros_like(node_ref)

    rank = rank_ref[river, pl.ds(tree, 1), :]
    value = ((rank & 127) + 128).astype(jnp.float32)
    for bit in range(6):
        value = jnp.where((rank & (128 << bit)) != 0, value * float(2 ** (2**bit)), value)
    phi[:, :hands] = jnp.broadcast_to(value, (8, hands))
    col[...] = jnp.broadcast_to(phi[0:1, :], (LANE, padded)).T.astype(jnp.bfloat16)

    following = jnp.minimum(step + 1, steps - 1)
    next_rows = rows_of(following)
    scale = rows_of(step)[0] / hands
    for n0 in range(0, padded, deep):
        nw = min(deep, padded - n0)
        row_phi = [phi[0:1, pl.ds(j, LANE)].astype(jnp.bfloat16) for j in range(n0, n0 + nw, LANE)]
        acc = jnp.zeros((2 * lines, nw), jnp.float32)
        for k0 in range(0, padded, deep):
            rows = pl.ds(k0, min(deep, padded - k0))
            parts = []
            for j in range(nw // LANE):
                gap = row_phi[j] - col[rows, :]
                cols = pl.ds(n0 + j * LANE, LANE)
                parts.append(jnp.maximum(jnp.minimum(gap, upper[rows, cols]), lower[rows, cols]))
            tile = jnp.concatenate(parts, axis=1)
            acc = acc + jnp.dot(stacked[:, rows], tile, preferred_element_type=jnp.float32)
        for start in range(n0, n0 + nw, LANE):
            prepare(following, next_rows, next_ref, start)
            width = min(LANE, hands - start)
            at = pl.ds(start, width)
            product = acc[:, start - n0 : start - n0 + width]
            scaled = scale[:, start : start + width]
            root_acc[:, at] += trav_ref[tree, :, at].astype(jnp.float32) * scaled * product[:lines]
            gain = scaled * product[lines:]
            node = gain * wgt[:, at]
            node_ref[0, :, at] += node
            for l in range(lines):
                plane = discount(regret_ref[0, l, :, at]) + potb[l, :, :width] * gain[l : l + 1]
                out_ref[0, l, :, at] = plane - node[l : l + 1]

    @pl.when(step == steps - 1)
    def _():
        root_ref[...] = jnp.sum(root_acc[...], axis=0, keepdims=True)


def run_local(turn_regret, river_regret, opp_reach, trav_reach, pot, blockers, ranks):
    trees, rivers, lines, _, hands = river_regret.shape
    steps = trees * rivers
    padded = -(-hands // LANE) * LANE
    inc = jnp.asarray(incidence(hands, padded), jnp.bfloat16)
    regrets = river_regret.reshape(steps, lines, lines, hands)
    bf, f32 = jnp.bfloat16, jnp.float32
    block = (1, lines, lines, hands)
    outs = pl.pallas_call(
        functools.partial(runout_kernel, hands, rivers, steps),
        grid=(steps,),
        out_shape=(
            jax.ShapeDtypeStruct(regrets.shape, f32),
            jax.ShapeDtypeStruct((trees, lines, hands), f32),
            jax.ShapeDtypeStruct((1, hands), f32),
        ),
        in_specs=[
            pl.BlockSpec(memory_space=pltpu.SMEM),
            pl.BlockSpec((padded, LANE), lambda i: (0, 0)),
            pl.BlockSpec(block, lambda i: (i, 0, 0, 0)),
            pl.BlockSpec(block, lambda i: (jnp.minimum(i + 1, steps - 1), 0, 0, 0)),
            pl.BlockSpec((trees, lines, hands), lambda i: (0, 0, 0)),
            pl.BlockSpec((trees, hands), lambda i: (0, 0)),
            pl.BlockSpec((trees, lines, hands), lambda i: (0, 0, 0)),
            pl.BlockSpec((rivers, trees, hands), lambda i: (0, 0, 0)),
            pl.BlockSpec((rivers, trees, hands), lambda i: (0, 0, 0)),
        ],
        out_specs=(
            pl.BlockSpec(block, lambda i: (i, 0, 0, 0)),
            pl.BlockSpec((1, lines, hands), lambda i: (i // rivers, 0, 0)),
            pl.BlockSpec((1, hands), lambda i: (0, 0)),
        ),
        scratch_shapes=[
            pltpu.VMEM((padded, padded), bf),
            pltpu.VMEM((padded, padded), bf),
            pltpu.VMEM((lines, lines, LANE), f32),
            pltpu.VMEM((2 * lines, padded), bf),
            pltpu.VMEM((lines, padded), f32),
            pltpu.VMEM((2 * lines, padded), bf),
            pltpu.VMEM((lines, padded), f32),
            pltpu.VMEM((8, padded), f32),
            pltpu.VMEM((padded, LANE), bf),
            pltpu.VMEM((lines, hands), f32),
        ],
        compiler_params=pltpu.CompilerParams(vmem_limit_bytes=60 * 2**20),
    )(pot, inc, regrets, regrets, turn_regret, opp_reach, trav_reach,
      blockers.transpose(1, 0, 2), ranks.transpose(1, 0, 2))
    return (outs[0].reshape(river_regret.shape),) + tuple(outs[1:])


def combine_kernel(
    line_size, turn_size, river_count, tree_count,
    node_ref, root_ref, turn_ref, out_ref, value_ref,
    outbox, inbox, total, gather, root_total, root_box, gain, strategy,
    send1, recv1, send2, recv2, send3, recv3,
):
    me, mine = lax.axis_index("line"), lax.axis_index("turn")
    line_peers = [lax.rem(me + i, line_size) for i in range(1, line_size)]
    turn_peers = [lax.rem(mine + i, turn_size) for i in range(1, turn_size)]
    mesh_ids = pl.DeviceIdType.MESH
    barrier = pltpu.get_barrier_semaphore()
    for peer in line_peers:
        pl.semaphore_signal(barrier, inc=1, device_id=(mine, peer), device_id_type=mesh_ids)
    for peer in turn_peers:
        pl.semaphore_signal(barrier, inc=1, device_id=(peer, me), device_id_type=mesh_ids)

    trees, lines, hands = node_ref.shape
    rows = trees * lines // line_size
    tiles = -(-hands // LANE)
    spans = [(j, min(LANE, hands - j * LANE)) for j in range(tiles)]
    outbox[...] = jnp.zeros_like(outbox)
    for j, width in spans:
        at = pl.ds(j * LANE, width)
        for d in range(line_size):
            tree, line = divmod(d * rows, lines)
            outbox[d, pl.ds(j * rows, rows), :width] = node_ref[tree, pl.ds(line, rows), at]
            outbox[d, pl.ds(tiles * rows + j, 1), :width] = root_ref[:, at]
    pl.semaphore_wait(barrier, line_size + turn_size - 2)

    firsts = []
    for peer in line_peers:
        copy = pltpu.make_async_remote_copy(
            src_ref=outbox.at[peer], dst_ref=inbox.at[me], send_sem=send1.at[peer],
            recv_sem=recv1.at[me], device_id=(mine, peer), device_id_type=mesh_ids,
        )
        copy.start()
        firsts.append(copy)
    inbox[me] = outbox[me]
    gain[...] = jnp.zeros_like(gain)
    for tree in range(trees):
        strategy[tree] = regret_match(turn_ref[tree], 0)
        out_ref[tree] = discount(turn_ref[tree])
    for peer in line_peers:
        pltpu.make_async_remote_copy(
            src_ref=outbox.at[peer], dst_ref=inbox.at[peer], send_sem=send1.at[peer],
            recv_sem=recv1.at[peer], device_id=(mine, peer), device_id_type=mesh_ids,
        ).wait_recv()
    summed = inbox[0]
    for d in range(1, line_size):
        summed = summed + inbox[d]
    total[...] = summed[: total.shape[0]]
    root_total[...] = jnp.zeros_like(root_total)
    root_total[:tiles, :] = summed[tiles * rows : tiles * rows + tiles]

    seconds = []
    for peer in line_peers:
        copy = pltpu.make_async_remote_copy(
            src_ref=total, dst_ref=gather.at[me], send_sem=send2.at[peer],
            recv_sem=recv2.at[me], device_id=(mine, peer), device_id_type=mesh_ids,
        )
        copy.start()
        seconds.append(copy)
    for peer in turn_peers:
        copy = pltpu.make_async_remote_copy(
            src_ref=root_total, dst_ref=root_box.at[mine], send_sem=send3.at[peer],
            recv_sem=recv3.at[mine], device_id=(peer, me), device_id_type=mesh_ids,
        )
        copy.start()
        seconds.append(copy)
    gather[me] = total[...]
    root_box[mine] = root_total[...]
    for peer in line_peers:
        pltpu.make_async_remote_copy(
            src_ref=total, dst_ref=gather.at[peer], send_sem=send2.at[peer],
            recv_sem=recv2.at[peer], device_id=(mine, peer), device_id_type=mesh_ids,
        ).wait_recv()
    for j, width in spans:
        for d in range(line_size):
            tree, line = divmod(d * rows, lines)
            gain[tree, pl.ds(line, rows), pl.ds(j * LANE, LANE)] = gather[d, pl.ds(j * rows, rows), :]
    for tree in range(trees):
        line_gain = gain[tree, :, :hands] / river_count
        average = jnp.sum(strategy[tree] * line_gain, axis=0, keepdims=True)
        out_ref[tree] = out_ref[tree] + line_gain - average
    for peer in turn_peers:
        pltpu.make_async_remote_copy(
            src_ref=root_total, dst_ref=root_box.at[peer], send_sem=send3.at[peer],
            recv_sem=recv3.at[peer], device_id=(peer, me), device_id_type=mesh_ids,
        ).wait_recv()
    value = root_box[0]
    for d in range(1, turn_size):
        value = value + root_box[d]
    value = value / (river_count * tree_count)
    for j, width in spans:
        value_ref[:, pl.ds(j * LANE, width)] = value[j : j + 1, :width]
    for copy in firsts + seconds:
        copy.wait_send()


def combine(node_sum, root, turn_regret, river_count, tree_count):
    trees, lines, hands = node_sum.shape
    line_size, turn_size = lax.axis_size("line"), lax.axis_size("turn")
    tiles = -(-hands // LANE)
    rows = trees * lines // line_size
    up8 = lambda n: -(-n // 8) * 8
    message, share, root_rows = up8(tiles * (rows + 1)), up8(tiles * rows), up8(tiles)
    f32, dma = jnp.float32, pltpu.SemaphoreType.DMA
    vmem = pl.BlockSpec(memory_space=pltpu.VMEM)
    return pl.pallas_call(
        functools.partial(combine_kernel, line_size, turn_size, river_count, tree_count),
        out_shape=(
            jax.ShapeDtypeStruct((trees, lines, hands), f32),
            jax.ShapeDtypeStruct((1, hands), f32),
        ),
        in_specs=[vmem] * 3,
        out_specs=(vmem, vmem),
        scratch_shapes=[
            pltpu.VMEM((line_size, message, LANE), f32),
            pltpu.VMEM((line_size, message, LANE), f32),
            pltpu.VMEM((share, LANE), f32),
            pltpu.VMEM((line_size, share, LANE), f32),
            pltpu.VMEM((root_rows, LANE), f32),
            pltpu.VMEM((turn_size, root_rows, LANE), f32),
            pltpu.VMEM((trees, lines, tiles * LANE), f32),
            pltpu.VMEM((trees, lines, hands), f32),
            dma((line_size,)), dma((line_size,)),
            dma((line_size,)), dma((line_size,)),
            dma((turn_size,)), dma((turn_size,)),
        ],
        compiler_params=pltpu.CompilerParams(
            collective_id=0, has_side_effects=True, vmem_limit_bytes=16 * 2**20
        ),
    )(node_sum, root, turn_regret)


def body(turn_regret, river_regret, opp_reach, trav_reach, pot, blockers, ranks):
    river_count = river_regret.shape[1] * lax.axis_size("line")
    tree_count = turn_regret.shape[0] * lax.axis_size("turn")
    new_river_regret, node_sum, root = run_local(
        turn_regret, river_regret, opp_reach, trav_reach, pot, blockers, ranks
    )
    new_turn_regret, root_value = combine(node_sum, root, turn_regret, river_count, tree_count)
    return (new_turn_regret, new_river_regret, root_value[0])


def solution(mesh):
    in_specs = (
        P("turn", None, None),
        P("turn", "line", None, None, None),
        P("turn", None),
        P("turn", None, None),
        P(),
        P("turn", "line", None),
        P("turn", "line", None),
    )
    out_specs = (P("turn", None, None), P("turn", "line", None, None, None), P())
    return jax.shard_map(body, mesh=mesh, in_specs=in_specs, out_specs=out_specs, check_vma=False)
```
